32 devices in a mesh: grp: 1, mon: 8 (over z, core), out: 4 (over y, x).
Axes of the slice: x: 2, y: 2, z: 4, core: 2. Of those that a mesh axis runs over, the one named last changes fastest.
Arguments:
- psi: float32 [2048, 512], P(('grp', 'mon', 'out')), may hold values from -6 to 6
- lodf: float32 [2048, 1024], P(('grp', 'mon'), 'out'), may hold values from -1 to 1
- block_map: int32 [16, 8], P(('grp', 'mon'), 'out'), may hold values 0 or 1
- margin: float32 [2048], P(('grp', 'mon')), may hold values from 1.5 to 4.5
- monitored: int32 [2048], P(('grp', 'mon')), may hold values from 0 to 2047, as said below
- outages: int32 [1024], P(('grp', 'out')), may hold values from 0 to 2047, as said below
Outputs:
- grad_psi: float32 [2048, 512], P(('grp', 'mon', 'out'))
The draws below stay inside these ranges and needn't reach their ends.
Inputs may be any that keep to these rules, and one draw needn't show every extreme that they name: Branch rows are in blocks of 64; block b is owned by index (b // 4, b % 4) of (mon, out). Entries i * 256 + j * 64 to i * 256 + (j + 1) * 64 - 1 of monitored are distinct rows of block i * 4 + j. Branch 0 and branch 2048 - 1 are always among them. Entries j * 256 + i * 32 to j * 256 + (i + 1) * 32 - 1 of outages are distinct rows of block i * 4 + j, with blocks owned as for monitored. Branch 0 and branch 2048 - 1 are always among them.
All inputs are finite; a program needn't handle non-finite values. No bound on the sum of `block_map` on one device may be relied on, other than what follows from the above.
Results may differ from the reference program's by a relative error of at most 0.0001.
Values sent between devices are 32-bit elements; how exact they have to be, the bound alone decides.
A program may use at most 64 MiB of HBM per device.

```python
import jax
import jax.numpy as jnp
from jax import lax

K = 512
BR_DEV = 64
SEL_M = 64
SEL_O = 32
LB = 128
BRANCHES = 2048
M = 2048
O = 1024
N_MON = 8
N_OUT = 4


def pick_rows(key, groups, members):
    scores = jax.random.randint(key, (groups, BR_DEV), 0, 1 << 20) * BR_DEV + jnp.arange(BR_DEV)[None, :]
    scores = scores.at[0, 0].set(-1).at[groups - 1, BR_DEV - 1].set(-1)
    order = jnp.argsort(scores, axis=1, stable=True)[:, :members]
    return order.astype(jnp.int32)


def draw_monitored(key, part):
    key = jax.random.fold_in(key, 11)
    local = pick_rows(key, N_MON * N_OUT, SEL_M).reshape(N_MON, N_OUT, SEL_M)
    block = jnp.arange(N_MON)[:, None, None] * N_OUT + jnp.arange(N_OUT)[None, :, None]
    return (block * BR_DEV + local).reshape(-1).astype(jnp.int32)


def draw_outages(key, part):
    key = jax.random.fold_in(key, 23)
    local = pick_rows(key, N_OUT * N_MON, SEL_O).reshape(N_OUT, N_MON, SEL_O)
    block = jnp.arange(N_MON)[None, :, None] * N_OUT + jnp.arange(N_OUT)[:, None, None]
    return (block * BR_DEV + local).reshape(-1).astype(jnp.int32)


def place_ends(array, key, low, top_value):
    longest = array.shape.index(max(array.shape))
    spots = []
    for shift in (0, 1):
        where = [jax.random.randint(jax.random.fold_in(key, axis), (), 0, length) for axis, length in enumerate(array.shape)]
        where[longest] = (where[longest] + shift) % array.shape[longest]
        spots.append(tuple(where))
    return array.at[spots[0]].set(low).at[spots[1]].set(top_value)


def level_of(rng, shape, cuts, smallest, largest):
    gain = 1.0
    for dim, blocks in cuts:
        steps = jax.random.uniform(jax.random.fold_in(jax.random.fold_in(rng, 6), dim), (blocks,), jnp.float32, smallest / len(cuts), largest / len(cuts))
        gain = gain * jnp.repeat(jnp.exp(steps), shape[dim] // blocks).reshape((-1,) + (1,) * (len(shape) - 1 - dim))
    return gain


def bell_draw(key, shape, deviation, bound, shards=(), held_as=jnp.bfloat16):
    gain = level_of(key, shape, shards, -0.22, 0.18) if shards else 1.0
    result = jax.random.normal(key, shape, jnp.float32) * deviation * gain
    return jnp.minimum(jnp.maximum(result, -bound), bound).astype(held_as)


def setup_inputs(seed: int = 0, part: int = 0) -> dict:
    streams_of = jax.random.split(jax.random.key(seed), 7)
    part_splits = jax.random.split(jax.random.fold_in(streams_of[6], part), 7)
    return {
        "psi": bell_draw(part_splits[0], (BRANCHES, K), 1.0, 6.0, ((0, 32),), jnp.float32),
        "lodf": jnp.clip(jax.random.uniform(part_splits[1], (M, O), jnp.float32, -1.0, 1.0) * level_of(part_splits[1], (M, O), ((0, 8), (1, 4)), -0.4, 0.0), -1.0, 1.0),
        "block_map": place_ends((jax.random.randint(part_splits[2], (M // LB, O // LB), 0, 4) < 3).astype(jnp.int32), jax.random.fold_in(part_splits[2], 1), 0, 1),
        "margin": jnp.clip(1.5 + 3.0 * jax.random.uniform(part_splits[3], (M,), jnp.float32) ** level_of(part_splits[3], (M,), ((0, 8),), -0.2, 0.2), 1.5, 4.5),
        "monitored": draw_monitored(jax.random.fold_in(jax.random.fold_in(streams_of[6], part), 71), part),
        "outages": draw_outages(jax.random.fold_in(jax.random.fold_in(streams_of[6], part), 71), part),
    }


def reference(psi, lodf, block_map, margin, monitored, outages):
    width = psi.shape[1]
    count_out = outages.shape[0]
    count_mon = monitored.shape[0]
    high = lax.Precision.HIGHEST
    psi_m = psi[monitored]
    psi_o = psi[outages]
    own_o = lax.optimization_barrier(jnp.sum(psi_o * psi_o, axis=1)) / width
    blocks = count_mon // LB
    rows_psi = psi_m.reshape(blocks, LB, width)
    rows_lodf = lodf.reshape(blocks, LB, count_out)
    rows_margin = margin.reshape(blocks, LB)
    mask_rows = jnp.repeat(block_map.astype(jnp.float32), LB, axis=1)

    def step(carry, item):
        adjoint, colsum = carry
        part_psi, part_lodf, part_margin, part_mask = item
        eff = part_lodf * part_mask[None, :]
        gram = jnp.dot(part_psi, psi_o.T, precision=high, preferred_element_type=jnp.float32) / width
        own_m = lax.optimization_barrier(jnp.sum(part_psi * part_psi, axis=1)) / width
        var = own_m[:, None] + 2.0 * eff * gram + eff * eff * own_o[None, :]
        sigma = jnp.sqrt(var + 1.0)
        q = jax.nn.sigmoid(2.0 * sigma - part_margin[:, None]) * 2.0 / (count_out * sigma)
        weighted = q * eff
        grad_m = lax.optimization_barrier(jnp.sum(q, axis=1))[:, None] * part_psi + jnp.dot(weighted, psi_o, precision=high, preferred_element_type=jnp.float32)
        adjoint = adjoint + jnp.dot(weighted.T, part_psi, precision=high, preferred_element_type=jnp.float32)
        colsum = colsum + lax.optimization_barrier(jnp.sum(q * eff * eff, axis=0))
        return ((adjoint, colsum), grad_m)
    start = (jnp.zeros((count_out, width), jnp.float32), jnp.zeros((count_out,), jnp.float32))
    (adjoint, colsum), grad_rows = lax.scan(step, start, (rows_psi, rows_lodf, rows_margin, mask_rows))
    grad_m = grad_rows.reshape(count_mon, width)
    grad_o = adjoint + colsum[:, None] * psi_o
    grad_psi = jnp.zeros(psi.shape, jnp.float32).at[monitored].add(grad_m).at[outages].add(grad_o)
    return grad_psi
```

```python
import functools

import jax
import jax.numpy as jnp
from jax import lax
from jax.experimental import pallas as pl
from jax.experimental.pallas import tpu as pltpu
from jax.sharding import PartitionSpec as P

BR_DEV = 64
SEL_M = 64
SEL_O = 32
LB = 128
OC = 256
MESH = pl.DeviceIdType.MESH
F32 = jnp.float32
BF16 = jnp.bfloat16


def split(a):
    hi = a.astype(BF16)
    return hi, (a - hi.astype(F32)).astype(BF16)


def dot3(a, b, dims):
    dn = (dims, ((), ()))
    dot = functools.partial(lax.dot_general, dimension_numbers=dn, preferred_element_type=F32)
    return dot(a[0], b[0]) + (dot(a[0], b[1]) + dot(a[1], b[0]))


def kernel(n_mon, n_out, scale,
           psi_hbm, lodf_ref, map_ref, margin_ref, mon_ref, outs_ref,
           out_ref,
           pv, pm, po, sel, selt, eff, marg, mpart, adj, rm, rs, rz,
           loc_sem, sm_s, sm_r, so_s, so_r, fw_s, rl_s, bm_s, bm_r, bs_s, bs_r, bz_s, bz_r):
    nz = n_mon // 2
    i = lax.axis_index("mon")
    j = lax.axis_index("out")
    z = i // 2
    c = lax.rem(i, 2)
    sib = i + 1 - 2 * c
    width = pm.shape[2]
    mon_count = n_out * SEL_M
    out_count = n_mon * SEL_O
    per = OC // SEL_O
    chunks = out_count // OC

    def to_out(d):
        return lax.rem(j + d, n_out)

    def from_out(d):
        return lax.rem(j + n_out - d, n_out)

    def to_z(d):
        return lax.rem(z + d, nz)

    def from_z(d):
        return lax.rem(z + nz - d, nz)

    def loop(count, f):
        if count <= 8:
            for d in range(count):
                f(d)
        else:
            lax.fori_loop(0, count, lambda d, x: (f(d), x)[1], 0)

    load = pltpu.make_async_copy(psi_hbm, pv, loc_sem)
    load.start()
    barrier = pltpu.get_barrier_semaphore()

    def sig_out(d):
        pl.semaphore_signal(barrier, inc=1, device_id={"out": to_out(d + 1)}, device_id_type=MESH)

    def sig_z(d):
        pl.semaphore_signal(barrier, inc=1, device_id={"mon": 2 * to_z(d + 1) + c}, device_id_type=MESH)

    loop(n_out - 1, sig_out)
    loop(nz - 1, sig_z)
    pl.semaphore_signal(barrier, inc=1, device_id={"mon": sib}, device_id_type=MESH)
    load.wait()
    for k in range(SEL_O):
        row = lax.rem(outs_ref[i * SEL_O + k], BR_DEV)
        sel[pl.ds(k, 1), :] = pv[pl.ds(row, 1), :]
    pl.semaphore_wait(barrier, n_out - 1 + nz - 1 + 1)

    def copy_m(d):
        return pltpu.make_async_remote_copy(
            pv, pm.at[j], sm_s.at[d], sm_r.at[j],
            device_id={"out": to_out(d + 1)}, device_id_type=MESH)

    def recv_m(d):
        s = from_out(d + 1)
        return pltpu.make_async_remote_copy(
            pv, pm.at[s], sm_s.at[d], sm_r.at[s],
            device_id={"out": to_out(d + 1)}, device_id_type=MESH)

    def copy_o(d):
        return pltpu.make_async_remote_copy(
            sel, po.at[i], so_s.at[d], so_r.at[i],
            device_id={"mon": 2 * to_z(d + 1) + c}, device_id_type=MESH)

    def copy_s():
        return pltpu.make_async_remote_copy(
            sel, po.at[i], fw_s, so_r.at[i],
            device_id={"mon": sib}, device_id_type=MESH)

    def from_slot(slot):
        return pltpu.make_async_remote_copy(
            sel, po.at[slot], fw_s, so_r.at[slot],
            device_id={"mon": sib}, device_id_type=MESH)

    def relay(d):
        slot = 2 * from_z(d + 1) + c
        return pltpu.make_async_remote_copy(
            po.at[slot], po.at[slot], rl_s.at[d], so_r.at[slot],
            device_id={"mon": sib}, device_id_type=MESH)

    loop(nz - 1, lambda d: copy_o(d).start())
    loop(n_out - 1, lambda d: copy_m(d).start())
    copy_s().start()
    po[i] = sel[...]
    pm[j] = pv[...]

    lane = lax.broadcasted_iota(jnp.int32, (1, BR_DEV), 1)
    for k in range(SEL_O):
        row = lax.rem(outs_ref[i * SEL_O + k], BR_DEV)
        selt[pl.ds(k, 1), :] = (lane == row).astype(F32)
    col = lax.broadcasted_iota(jnp.int32, (1, mon_count), 1)
    place = col // SEL_M * BR_DEV + lax.rem(mon_ref[...], BR_DEV)
    hit = lax.broadcasted_iota(jnp.int32, (mon_count, mon_count), 0) == place
    marg[...] = jnp.sum(jnp.where(hit, margin_ref[...], 0.0), axis=1, keepdims=True)
    perm = hit.astype(BF16)

    def lay(ch, _):
        if chunks == 1:
            cols = slice(0, OC)
        else:
            cols = pl.ds(pl.multiple_of(ch * OC, OC), OC)
        lf = lodf_ref[:, cols]
        parts = []
        for a in range(mon_count // LB):
            parts.append(jnp.concatenate(
                [lf[a * LB:(a + 1) * LB, b * LB:(b + 1) * LB] * map_ref[a, ch * (OC // LB) + b].astype(F32)
                 for b in range(OC // LB)], axis=1))
        e = jnp.concatenate(parts, axis=0)
        e0 = e.astype(BF16)
        r1 = e - e0.astype(F32)
        e1 = r1.astype(BF16)
        e2 = (r1 - e1.astype(F32)).astype(BF16)
        dot = functools.partial(jnp.dot, preferred_element_type=F32)
        eff[:, cols] = dot(perm, e0) + (dot(perm, e1) + dot(perm, e2))
        return 0

    if chunks == 1:
        lay(0, 0)
    else:
        lax.fori_loop(0, chunks, lay, 0)

    def take_z(d):
        slot = 2 * from_z(d + 1) + c
        from_slot(slot).wait_recv()
        relay(d).start()

    loop(nz - 1, take_z)
    loop(n_out - 1, lambda d: recv_m(d).wait_recv())
    from_slot(sib).wait_recv()
    loop(nz - 1, lambda d: from_slot(2 * from_z(d + 1) + 1 - c).wait_recv())

    psi_m = pm[...].reshape(mon_count, width)
    m2 = split(psi_m)
    own_m = jnp.sum(psi_m * psi_m, axis=1, keepdims=True) * (1.0 / width)
    margin = marg[...]
    ones_o = jnp.ones((8, width), BF16)
    ones_m = jnp.ones((mon_count, 128), BF16)

    def compute(ch, _):
        if chunks == 1:
            cols = slice(0, OC)
            rows = slice(0, per)
        else:
            cols = pl.ds(pl.multiple_of(ch * OC, OC), OC)
            rows = pl.ds(ch * per, per)
        psi_o = po[rows].reshape(OC, width)
        o2 = split(psi_o)
        gram = dot3(m2, o2, ((1,), (1,))) * (1.0 / width)
        s2 = split(psi_o * psi_o)
        dn = (((1,), (1,)), ((), ()))
        own_o = (lax.dot_general(ones_o, s2[0], dn, preferred_element_type=F32)
                 + lax.dot_general(ones_o, s2[1], dn, preferred_element_type=F32))[0:1] * (1.0 / width)
        e = eff[:, cols]
        var1 = (own_m + 1.0) + e * (2.0 * gram + e * own_o)
        inv = lax.rsqrt(var1)
        q = inv * scale / (1.0 + jnp.exp(margin - 2.0 * (var1 * inv)))
        w = q * e
        w2 = split(w)
        part = dot3(w2, o2, ((1,), (0,))) + jnp.sum(q, axis=1, keepdims=True) * psi_m
        part = part.reshape(n_out, SEL_M, width)
        if chunks == 1:
            mpart[...] = part
        else:
            @pl.when(ch == 0)
            def _():
                mpart[...] = part

            @pl.when(ch > 0)
            def _():
                mpart[...] += part
        c2 = split(w * e)
        dn0 = (((0,), (0,)), ((), ()))
        colsum = (lax.dot_general(c2[0], ones_m, dn0, preferred_element_type=F32)
                  + lax.dot_general(c2[1], ones_m, dn0, preferred_element_type=F32))[:, 0:1]
        a = dot3(w2, m2, ((0,), (0,))) + colsum * psi_o
        a = a.reshape(per, SEL_O, width)
        for b in range(per):
            adj[b % 2, ch * (per // 2) + b // 2] = a[b]
        return 0

    if chunks == 1:
        compute(0, 0)
    else:
        lax.fori_loop(0, chunks, compute, 0)

    def sib_copy(d):
        zz = to_z(d)
        return pltpu.make_async_remote_copy(
            adj.at[1 - c, zz], rs.at[zz], bs_s.at[zz], bs_r.at[zz],
            device_id={"mon": sib}, device_id_type=MESH)

    def z_copy(d):
        zz = to_z(d)
        return pltpu.make_async_remote_copy(
            adj.at[c, zz], rz.at[z], bz_s.at[d], bz_r.at[z],
            device_id={"mon": 2 * zz + c}, device_id_type=MESH)

    def z_recv(d):
        zz = from_z(d)
        return pltpu.make_async_remote_copy(
            adj.at[c, zz], rz.at[zz], bz_s.at[d], bz_r.at[zz],
            device_id={"mon": 2 * zz + c}, device_id_type=MESH)

    def b_copy(d):
        p = to_out(d + 1)
        return pltpu.make_async_remote_copy(
            mpart.at[p], rm.at[j], bm_s.at[d], bm_r.at[j],
            device_id={"out": p}, device_id_type=MESH)

    def b_recv(d):
        s = from_out(d + 1)
        return pltpu.make_async_remote_copy(
            mpart.at[s], rm.at[s], bm_s.at[d], bm_r.at[s],
            device_id={"out": s}, device_id_type=MESH)

    loop(nz, lambda d: sib_copy((d + 1) % nz if isinstance(d, int) else lax.rem(d + 1, nz)).start())
    loop(n_out - 1, lambda d: b_copy(d).start())

    def pass_z(d):
        zz = to_z(d + 1)
        sib_copy(d + 1).wait_recv()
        adj[c, zz] = adj[c, zz] + rs[zz]
        z_copy(d + 1).start()

    loop(nz - 1, pass_z)
    sib_copy(0).wait_recv()
    rz[z] = adj[c, z] + rs[z]

    loop(nz - 1, lambda d: z_recv(d + 1).wait_recv())
    if nz <= 8:
        tot = rz[z]
        for d in range(1, nz):
            tot = tot + rz[from_z(d)]
    else:
        tot = lax.fori_loop(1, nz, lambda d, t: t + rz[from_z(d)], rz[z])
    t0 = tot.astype(BF16)
    r1 = tot - t0.astype(F32)
    t1 = r1.astype(BF16)
    t2 = (r1 - t1.astype(F32)).astype(BF16)
    st = selt[...].astype(BF16)
    dn0 = (((0,), (0,)), ((), ()))
    put = functools.partial(lax.dot_general, dimension_numbers=dn0, preferred_element_type=F32)
    res = put(st, t0) + (put(st, t1) + put(st, t2)) + mpart[j]
    for d in range(n_out - 1):
        b_recv(d).wait_recv()
        res = res + rm[from_out(d + 1)]
    out_ref[...] = res

    loop(nz - 1, lambda d: copy_o(d).wait_send())
    loop(n_out - 1, lambda d: copy_m(d).wait_send())
    copy_s().wait_send()
    loop(nz - 1, lambda d: relay(d).wait_send())
    loop(nz, lambda d: sib_copy(d).wait_send())
    loop(nz - 1, lambda d: z_copy(d + 1).wait_send())
    loop(n_out - 1, lambda d: b_copy(d).wait_send())


def body(n_mon, n_out, psi, lodf, block_map, margin, monitored, outages):
    width = psi.shape[1]
    mon_count = monitored.shape[0]
    out_count = outages.shape[0]
    nz = n_mon // 2
    total_out = out_count * n_out
    vm = pl.BlockSpec(memory_space=pltpu.VMEM)
    sm = pl.BlockSpec(memory_space=pltpu.SMEM)
    dma = pltpu.SemaphoreType.DMA
    return pl.pallas_call(
        functools.partial(kernel, n_mon, n_out, 2.0 / total_out),
        out_shape=jax.ShapeDtypeStruct(psi.shape, F32),
        in_specs=[pl.BlockSpec(memory_space=pl.ANY), vm, sm, vm, vm, sm],
        out_specs=vm,
        scratch_shapes=[
            pltpu.VMEM(psi.shape, F32),
            pltpu.VMEM((n_out, BR_DEV, width), F32),
            pltpu.VMEM((n_mon, SEL_O, width), F32),
            pltpu.VMEM((SEL_O, width), F32),
            pltpu.VMEM((SEL_O, BR_DEV), F32),
            pltpu.VMEM((mon_count, out_count), F32),
            pltpu.VMEM((mon_count, 1), F32),
            pltpu.VMEM((n_out, BR_DEV, width), F32),
            pltpu.VMEM((2, nz, SEL_O, width), F32),
            pltpu.VMEM((n_out, BR_DEV, width), F32),
            pltpu.VMEM((nz, SEL_O, width), F32),
            pltpu.VMEM((nz, SEL_O, width), F32),
            dma(()), dma((n_out - 1,)), dma((n_out,)), dma((nz,)), dma((n_mon,)),
            dma(()), dma((nz,)), dma((n_out - 1,)), dma((n_out,)),
            dma((nz,)), dma((nz,)), dma((nz,)), dma((nz,)),
        ],
        compiler_params=pltpu.CompilerParams(
            collective_id=0, has_side_effects=True, vmem_limit_bytes=40 << 20),
        name="flow_variance_grad",
    )(psi, lodf, block_map, margin.reshape(1, -1), monitored.reshape(1, -1), outages)


def solution(mesh):
    in_specs = (
        P(("grp", "mon", "out"), None),
        P(("grp", "mon"), "out"),
        P(("grp", "mon"), "out"),
        P(("grp", "mon")),
        P(("grp", "mon")),
        P(("grp", "out")),
    )
    out_specs = P(("grp", "mon", "out"), None)
    fn = functools.partial(body, mesh.shape["mon"], mesh.shape["out"])
    return jax.shard_map(fn, mesh=mesh, in_specs=in_specs, out_specs=out_specs, check_vma=False)
```

```python
import functools

import jax
import jax.numpy as jnp
from jax import lax
from jax.experimental import pallas as pl
from jax.experimental.pallas import tpu as pltpu
from jax.sharding import PartitionSpec as P

BR_DEV = 64
SEL_M = 64
SEL_O = 32
LB = 128
OC = 256
MESH = pl.DeviceIdType.MESH
F32 = jnp.float32
BF16 = jnp.bfloat16


def split(a):
    hi = a.astype(BF16)
    return hi, (a - hi.astype(F32)).astype(BF16)


def dot3(a, b, dims):
    dn = (dims, ((), ()))
    dot = functools.partial(lax.dot_general, dimension_numbers=dn, preferred_element_type=F32)
    return dot(a[0], b[0]) + (dot(a[0], b[1]) + dot(a[1], b[0]))


def kernel(n_mon, n_out, scale,
           psi_hbm, lodf_hbm, map_hbm, margin_hbm, mon_hbm, outs_hbm,
           out_ref,
           lodf_ref, map_ref, margin_ref, mon_ref, outs_ref,
           pv, pm, po, sel, selt, eff, marg, mpart, adj, rm, rs, rz,
           loc_sem, sm_s, sm_r, so_s, so_r, fw_s, rl_s, bm_s, bm_r, bs_s, bs_r, bz_s, bz_r):
    nz = n_mon // 2
    i = lax.axis_index("mon")
    j = lax.axis_index("out")
    z = i // 2
    c = lax.rem(i, 2)
    sib = i + 1 - 2 * c
    width = pm.shape[2]
    mon_count = n_out * SEL_M
    out_count = n_mon * SEL_O
    per = OC // SEL_O
    chunks = out_count // OC

    def to_out(d):
        return lax.rem(j + d, n_out)

    def from_out(d):
        return lax.rem(j + n_out - d, n_out)

    def to_z(d):
        return lax.rem(z + d, nz)

    def from_z(d):
        return lax.rem(z + nz - d, nz)

    def loop(count, f):
        if count <= 8:
            for d in range(count):
                f(d)
        else:
            lax.fori_loop(0, count, lambda d, x: (f(d), x)[1], 0)

    loads = [pltpu.make_async_copy(a, b, loc_sem.at[k]) for k, (a, b) in enumerate([
        (outs_hbm, outs_ref), (psi_hbm, pv), (mon_hbm, mon_ref),
        (margin_hbm, margin_ref), (map_hbm, map_ref), (lodf_hbm, lodf_ref)])]
    for load in loads:
        load.start()
    barrier = pltpu.get_barrier_semaphore()

    def sig_out(d):
        pl.semaphore_signal(barrier, inc=1, device_id={"out": to_out(d + 1)}, device_id_type=MESH)

    def sig_z(d):
        pl.semaphore_signal(barrier, inc=1, device_id={"mon": 2 * to_z(d + 1) + c}, device_id_type=MESH)

    loop(n_out - 1, sig_out)
    loop(nz - 1, sig_z)
    pl.semaphore_signal(barrier, inc=1, device_id={"mon": sib}, device_id_type=MESH)
    loads[0].wait()
    loads[1].wait()
    for k in range(SEL_O):
        row = lax.rem(outs_ref[i * SEL_O + k], BR_DEV)
        sel[pl.ds(k, 1), :] = pv[pl.ds(row, 1), :]
    pl.semaphore_wait(barrier, n_out - 1 + nz - 1 + 1)

    def copy_m(d):
        return pltpu.make_async_remote_copy(
            pv, pm.at[j], sm_s.at[d], sm_r.at[j],
            device_id={"out": to_out(d + 1)}, device_id_type=MESH)

    def recv_m(d):
        s = from_out(d + 1)
        return pltpu.make_async_remote_copy(
            pv, pm.at[s], sm_s.at[d], sm_r.at[s],
            device_id={"out": to_out(d + 1)}, device_id_type=MESH)

    def copy_o(d):
        return pltpu.make_async_remote_copy(
            sel, po.at[i], so_s.at[d], so_r.at[i],
            device_id={"mon": 2 * to_z(d + 1) + c}, device_id_type=MESH)

    def copy_s():
        return pltpu.make_async_remote_copy(
            sel, po.at[i], fw_s, so_r.at[i],
            device_id={"mon": sib}, device_id_type=MESH)

    def from_slot(slot):
        return pltpu.make_async_remote_copy(
            sel, po.at[slot], fw_s, so_r.at[slot],
            device_id={"mon": sib}, device_id_type=MESH)

    def relay(d):
        slot = 2 * from_z(d + 1) + c
        return pltpu.make_async_remote_copy(
            po.at[slot], po.at[slot], rl_s.at[d], so_r.at[slot],
            device_id={"mon": sib}, device_id_type=MESH)

    loop(nz - 1, lambda d: copy_o(d).start())
    loop(n_out - 1, lambda d: copy_m(d).start())
    copy_s().start()
    po[i] = sel[...]
    pm[j] = pv[...]

    lane = lax.broadcasted_iota(jnp.int32, (1, BR_DEV), 1)
    for k in range(SEL_O):
        row = lax.rem(outs_ref[i * SEL_O + k], BR_DEV)
        selt[pl.ds(k, 1), :] = (lane == row).astype(F32)
    for load in loads[2:]:
        load.wait()
    col = lax.broadcasted_iota(jnp.int32, (1, mon_count), 1)
    place = col // SEL_M * BR_DEV + lax.rem(mon_ref[...], BR_DEV)
    hit = lax.broadcasted_iota(jnp.int32, (mon_count, mon_count), 0) == place
    marg[...] = jnp.sum(jnp.where(hit, margin_ref[...], 0.0), axis=1, keepdims=True)
    perm = hit.astype(BF16)

    def lay(ch, _):
        if chunks == 1:
            cols = slice(0, OC)
        else:
            cols = pl.ds(pl.multiple_of(ch * OC, OC), OC)
        lf = lodf_ref[:, cols]
        parts = []
        for a in range(mon_count // LB):
            parts.append(jnp.concatenate(
                [lf[a * LB:(a + 1) * LB, b * LB:(b + 1) * LB] * map_ref[a, ch * (OC // LB) + b].astype(F32)
                 for b in range(OC // LB)], axis=1))
        e = jnp.concatenate(parts, axis=0)
        e0 = e.astype(BF16)
        r1 = e - e0.astype(F32)
        e1 = r1.astype(BF16)
        e2 = (r1 - e1.astype(F32)).astype(BF16)
        dot = functools.partial(jnp.dot, preferred_element_type=F32)
        eff[:, cols] = dot(perm, e0) + (dot(perm, e1) + dot(perm, e2))
        return 0

    if chunks == 1:
        lay(0, 0)
    else:
        lax.fori_loop(0, chunks, lay, 0)

    def take_z(d):
        slot = 2 * from_z(d + 1) + c
        from_slot(slot).wait_recv()
        relay(d).start()

    loop(nz - 1, take_z)
    loop(n_out - 1, lambda d: recv_m(d).wait_recv())
    from_slot(sib).wait_recv()
    loop(nz - 1, lambda d: from_slot(2 * from_z(d + 1) + 1 - c).wait_recv())

    psi_m = pm[...].reshape(mon_count, width)
    m2 = split(psi_m)
    own_m = jnp.sum(psi_m * psi_m, axis=1, keepdims=True) * (1.0 / width)
    margin = marg[...]
    ones_o = jnp.ones((8, width), BF16)
    ones_m = jnp.ones((mon_count, 128), BF16)

    def compute(ch, _):
        if chunks == 1:
            cols = slice(0, OC)
            rows = slice(0, per)
        else:
            cols = pl.ds(pl.multiple_of(ch * OC, OC), OC)
            rows = pl.ds(ch * per, per)
        psi_o = po[rows].reshape(OC, width)
        o2 = split(psi_o)
        gram = dot3(m2, o2, ((1,), (1,))) * (1.0 / width)
        s2 = split(psi_o * psi_o)
        dn = (((1,), (1,)), ((), ()))
        own_o = (lax.dot_general(ones_o, s2[0], dn, preferred_element_type=F32)
                 + lax.dot_general(ones_o, s2[1], dn, preferred_element_type=F32))[0:1] * (1.0 / width)
        e = eff[:, cols]
        var1 = (own_m + 1.0) + e * (2.0 * gram + e * own_o)
        inv = lax.rsqrt(var1)
        q = inv * scale / (1.0 + jnp.exp(margin - 2.0 * (var1 * inv)))
        w = q * e
        w2 = split(w)
        part = dot3(w2, o2, ((1,), (0,))) + jnp.sum(q, axis=1, keepdims=True) * psi_m
        part = part.reshape(n_out, SEL_M, width)
        if chunks == 1:
            mpart[...] = part
        else:
            @pl.when(ch == 0)
            def _():
                mpart[...] = part

            @pl.when(ch > 0)
            def _():
                mpart[...] += part
        c2 = split(w * e)
        dn0 = (((0,), (0,)), ((), ()))
        colsum = (lax.dot_general(c2[0], ones_m, dn0, preferred_element_type=F32)
                  + lax.dot_general(c2[1], ones_m, dn0, preferred_element_type=F32))[:, 0:1]
        a = dot3(w2, m2, ((0,), (0,))) + colsum * psi_o
        a = a.reshape(per, SEL_O, width)
        for b in range(per):
            adj[b % 2, ch * (per // 2) + b // 2] = a[b]
        return 0

    if chunks == 1:
        compute(0, 0)
    else:
        lax.fori_loop(0, chunks, compute, 0)

    def sib_copy(d):
        zz = to_z(d)
        return pltpu.make_async_remote_copy(
            adj.at[1 - c, zz], rs.at[zz], bs_s.at[zz], bs_r.at[zz],
            device_id={"mon": sib}, device_id_type=MESH)

    def z_copy(d):
        zz = to_z(d)
        return pltpu.make_async_remote_copy(
            adj.at[c, zz], rz.at[z], bz_s.at[d], bz_r.at[z],
            device_id={"mon": 2 * zz + c}, device_id_type=MESH)

    def z_recv(d):
        zz = from_z(d)
        return pltpu.make_async_remote_copy(
            adj.at[c, zz], rz.at[zz], bz_s.at[d], bz_r.at[zz],
            device_id={"mon": 2 * zz + c}, device_id_type=MESH)

    def b_copy(d):
        p = to_out(d + 1)
        return pltpu.make_async_remote_copy(
            mpart.at[p], rm.at[j], bm_s.at[d], bm_r.at[j],
            device_id={"out": p}, device_id_type=MESH)

    def b_recv(d):
        s = from_out(d + 1)
        return pltpu.make_async_remote_copy(
            mpart.at[s], rm.at[s], bm_s.at[d], bm_r.at[s],
            device_id={"out": s}, device_id_type=MESH)

    loop(nz, lambda d: sib_copy((d + 1) % nz if isinstance(d, int) else lax.rem(d + 1, nz)).start())
    loop(n_out - 1, lambda d: b_copy(d).start())

    def pass_z(d):
        zz = to_z(d + 1)
        sib_copy(d + 1).wait_recv()
        adj[c, zz] = adj[c, zz] + rs[zz]
        z_copy(d + 1).start()

    loop(nz - 1, pass_z)
    sib_copy(0).wait_recv()
    rz[z] = adj[c, z] + rs[z]

    loop(nz - 1, lambda d: z_recv(d + 1).wait_recv())
    if nz <= 8:
        tot = rz[z]
        for d in range(1, nz):
            tot = tot + rz[from_z(d)]
    else:
        tot = lax.fori_loop(1, nz, lambda d, t: t + rz[from_z(d)], rz[z])
    t0 = tot.astype(BF16)
    r1 = tot - t0.astype(F32)
    t1 = r1.astype(BF16)
    t2 = (r1 - t1.astype(F32)).astype(BF16)
    st = selt[...].astype(BF16)
    dn0 = (((0,), (0,)), ((), ()))
    put = functools.partial(lax.dot_general, dimension_numbers=dn0, preferred_element_type=F32)
    res = put(st, t0) + (put(st, t1) + put(st, t2)) + mpart[j]
    for d in range(n_out - 1):
        b_recv(d).wait_recv()
        res = res + rm[from_out(d + 1)]
    out_ref[...] = res

    loop(nz - 1, lambda d: copy_o(d).wait_send())
    loop(n_out - 1, lambda d: copy_m(d).wait_send())
    copy_s().wait_send()
    loop(nz - 1, lambda d: relay(d).wait_send())
    loop(nz, lambda d: sib_copy(d).wait_send())
    loop(nz - 1, lambda d: z_copy(d + 1).wait_send())
    loop(n_out - 1, lambda d: b_copy(d).wait_send())


def body(n_mon, n_out, psi, lodf, block_map, margin, monitored, outages):
    width = psi.shape[1]
    mon_count = monitored.shape[0]
    out_count = outages.shape[0]
    nz = n_mon // 2
    total_out = out_count * n_out
    vm = pl.BlockSpec(memory_space=pltpu.VMEM)
    dma = pltpu.SemaphoreType.DMA
    return pl.pallas_call(
        functools.partial(kernel, n_mon, n_out, 2.0 / total_out),
        out_shape=jax.ShapeDtypeStruct(psi.shape, F32),
        in_specs=[pl.BlockSpec(memory_space=pl.ANY)] * 6,
        out_specs=vm,
        scratch_shapes=[
            pltpu.VMEM(lodf.shape, F32),
            pltpu.SMEM(block_map.shape, jnp.int32),
            pltpu.VMEM((1, mon_count), F32),
            pltpu.VMEM((1, mon_count), jnp.int32),
            pltpu.SMEM(outages.shape, jnp.int32),
            pltpu.VMEM(psi.shape, F32),
            pltpu.VMEM((n_out, BR_DEV, width), F32),
            pltpu.VMEM((n_mon, SEL_O, width), F32),
            pltpu.VMEM((SEL_O, width), F32),
            pltpu.VMEM((SEL_O, BR_DEV), F32),
            pltpu.VMEM((mon_count, out_count), F32),
            pltpu.VMEM((mon_count, 1), F32),
            pltpu.VMEM((n_out, BR_DEV, width), F32),
            pltpu.VMEM((2, nz, SEL_O, width), F32),
            pltpu.VMEM((n_out, BR_DEV, width), F32),
            pltpu.VMEM((nz, SEL_O, width), F32),
            pltpu.VMEM((nz, SEL_O, width), F32),
            dma((6,)), dma((n_out - 1,)), dma((n_out,)), dma((nz,)), dma((n_mon,)),
            dma(()), dma((nz,)), dma((n_out - 1,)), dma((n_out,)),
            dma((nz,)), dma((nz,)), dma((nz,)), dma((nz,)),
        ],
        compiler_params=pltpu.CompilerParams(
            collective_id=0, has_side_effects=True, vmem_limit_bytes=60 << 20),
        name="flow_variance_grad",
    )(psi, lodf, block_map, margin.reshape(1, -1), monitored.reshape(1, -1), outages)


def solution(mesh):
    in_specs = (
        P(("grp", "mon", "out"), None),
        P(("grp", "mon"), "out"),
        P(("grp", "mon"), "out"),
        P(("grp", "mon")),
        P(("grp", "mon")),
        P(("grp", "out")),
    )
    out_specs = P(("grp", "mon", "out"), None)
    fn = functools.partial(body, mesh.shape["mon"], mesh.shape["out"])
    return jax.shard_map(fn, mesh=mesh, in_specs=in_specs, out_specs=out_specs, check_vma=False)
```

```python
import functools

import jax
import jax.numpy as jnp
from jax import lax
from jax.experimental import pallas as pl
from jax.experimental.pallas import tpu as pltpu
from jax.sharding import PartitionSpec as P

BR_DEV = 64
SEL_M = 64
SEL_O = 32
LB = 128
OC = 256
MESH = pl.DeviceIdType.MESH
F32 = jnp.float32
BF16 = jnp.bfloat16


def split(a):
    hi = a.astype(BF16)
    return hi, (a - hi.astype(F32)).astype(BF16)


def dot3(a, b, dims):
    dn = (dims, ((), ()))
    dot = functools.partial(lax.dot_general, dimension_numbers=dn, preferred_element_type=F32)
    return dot(a[0], b[0]) + (dot(a[0], b[1]) + dot(a[1], b[0]))


def kernel(n_mon, n_out, scale,
           psi_hbm, lodf_hbm, map_hbm, margin_hbm, mon_hbm, outs_hbm,
           out_ref,
           lodf_ref, map_ref, margin_ref, mon_ref, outs_ref,
           pv, pm, po, sel, selt, eff, marg, mpart, adj, rm, rs, rz,
           loc_sem, sm_s, sm_r, so_s, so_r, fw_s, rl_s, bm_s, bm_r, bs_s, bs_r, bz_s, bz_r):
    nz = n_mon // 2
    i = lax.axis_index("mon")
    j = lax.axis_index("out")
    z = i // 2
    c = lax.rem(i, 2)
    sib = i + 1 - 2 * c
    width = pm.shape[2]
    mon_count = n_out * SEL_M
    out_count = n_mon * SEL_O
    per = OC // SEL_O
    chunks = out_count // OC

    def to_out(d):
        return lax.rem(j + d, n_out)

    def from_out(d):
        return lax.rem(j + n_out - d, n_out)

    def to_z(d):
        return lax.rem(z + d, nz)

    def from_z(d):
        return lax.rem(z + nz - d, nz)

    def loop(count, f):
        if count <= 8:
            for d in range(count):
                f(d)
        else:
            lax.fori_loop(0, count, lambda d, x: (f(d), x)[1], 0)

    loads = [pltpu.make_async_copy(a, b, loc_sem.at[k]) for k, (a, b) in enumerate([
        (outs_hbm, outs_ref), (psi_hbm, pv), (mon_hbm, mon_ref),
        (margin_hbm, margin_ref), (map_hbm, map_ref), (lodf_hbm, lodf_ref)])]
    for load in loads:
        load.start()
    barrier = pltpu.get_barrier_semaphore()

    def sig_out(d):
        pl.semaphore_signal(barrier, inc=1, device_id={"out": to_out(d + 1)}, device_id_type=MESH)

    def sig_z(d):
        pl.semaphore_signal(barrier, inc=1, device_id={"mon": 2 * to_z(d + 1) + c}, device_id_type=MESH)

    loop(n_out - 1, sig_out)
    loop(nz - 1, sig_z)
    pl.semaphore_signal(barrier, inc=1, device_id={"mon": sib}, device_id_type=MESH)
    loads[0].wait()
    loads[1].wait()
    for k in range(SEL_O):
        row = lax.rem(outs_ref[i * SEL_O + k], BR_DEV)
        sel[pl.ds(k, 1), :] = pv[pl.ds(row, 1), :]
    pl.semaphore_wait(barrier, n_out - 1 + nz - 1 + 1)

    def copy_m(d):
        return pltpu.make_async_remote_copy(
            pv, pm.at[j], sm_s.at[d], sm_r.at[j],
            device_id={"out": to_out(d + 1)}, device_id_type=MESH)

    def recv_m(d):
        s = from_out(d + 1)
        return pltpu.make_async_remote_copy(
            pv, pm.at[s], sm_s.at[d], sm_r.at[s],
            device_id={"out": to_out(d + 1)}, device_id_type=MESH)

    def copy_o(d):
        return pltpu.make_async_remote_copy(
            sel, po.at[i], so_s.at[d], so_r.at[i],
            device_id={"mon": 2 * to_z(d + 1) + c}, device_id_type=MESH)

    def copy_s():
        return pltpu.make_async_remote_copy(
            sel, po.at[i], fw_s, so_r.at[i],
            device_id={"mon": sib}, device_id_type=MESH)

    def from_slot(slot):
        return pltpu.make_async_remote_copy(
            sel, po.at[slot], fw_s, so_r.at[slot],
            device_id={"mon": sib}, device_id_type=MESH)

    def relay(d):
        slot = 2 * from_z(d + 1) + c
        return pltpu.make_async_remote_copy(
            po.at[slot], po.at[slot], rl_s.at[d], so_r.at[slot],
            device_id={"mon": sib}, device_id_type=MESH)

    loop(nz - 1, lambda d: copy_o(d).start())
    loop(n_out - 1, lambda d: copy_m(d).start())
    copy_s().start()
    po[i] = sel[...]
    pm[j] = pv[...]

    lane = lax.broadcasted_iota(jnp.int32, (1, BR_DEV), 1)
    for k in range(SEL_O):
        row = lax.rem(outs_ref[i * SEL_O + k], BR_DEV)
        selt[pl.ds(k, 1), :] = (lane == row).astype(F32)
    for load in loads[2:]:
        load.wait()
    col = lax.broadcasted_iota(jnp.int32, (1, mon_count), 1)
    place = col // SEL_M * BR_DEV + lax.rem(mon_ref[...], BR_DEV)
    hit = lax.broadcasted_iota(jnp.int32, (mon_count, mon_count), 0) == place
    marg[...] = jnp.sum(jnp.where(hit, margin_ref[...], 0.0), axis=1, keepdims=True)
    perm = hit.astype(BF16)

    def lay(ch, _):
        if chunks == 1:
            cols = slice(0, OC)
        else:
            cols = pl.ds(pl.multiple_of(ch * OC, OC), OC)
        lf = lodf_ref[:, cols]
        parts = []
        for a in range(mon_count // LB):
            parts.append(jnp.concatenate(
                [lf[a * LB:(a + 1) * LB, b * LB:(b + 1) * LB] * map_ref[a, ch * (OC // LB) + b].astype(F32)
                 for b in range(OC // LB)], axis=1))
        e = jnp.concatenate(parts, axis=0)
        e0 = e.astype(BF16)
        r1 = e - e0.astype(F32)
        e1 = r1.astype(BF16)
        e2 = (r1 - e1.astype(F32)).astype(BF16)
        dot = functools.partial(jnp.dot, preferred_element_type=F32)
        eff[:, cols] = dot(perm, e0) + (dot(perm, e1) + dot(perm, e2))
        return 0

    if chunks == 1:
        lay(0, 0)
    else:
        lax.fori_loop(0, chunks, lay, 0)

    def take_z(d):
        slot = 2 * from_z(d + 1) + c
        from_slot(slot).wait_recv()
        relay(d).start()

    loop(nz - 1, take_z)
    loop(n_out - 1, lambda d: recv_m(d).wait_recv())
    from_slot(sib).wait_recv()
    loop(nz - 1, lambda d: from_slot(2 * from_z(d + 1) + 1 - c).wait_recv())

    psi_m = pm[...].reshape(mon_count, width)
    m2 = split(psi_m)
    own_m = jnp.sum(psi_m * psi_m, axis=1, keepdims=True) * (1.0 / width)
    margin = marg[...]
    ones_o = jnp.ones((8, width), BF16)
    ones_m = jnp.ones((mon_count, 128), BF16)

    def compute(ch, _):
        if chunks == 1:
            cols = slice(0, OC)
            rows = slice(0, per)
        else:
            cols = pl.ds(pl.multiple_of(ch * OC, OC), OC)
            rows = pl.ds(ch * per, per)
        psi_o = po[rows].reshape(OC, width)
        o2 = split(psi_o)
        gram = dot3(m2, o2, ((1,), (1,))) * (1.0 / width)
        s2 = split(psi_o * psi_o)
        dn = (((1,), (1,)), ((), ()))
        own_o = (lax.dot_general(ones_o, s2[0], dn, preferred_element_type=F32)
                 + lax.dot_general(ones_o, s2[1], dn, preferred_element_type=F32))[0:1] * (1.0 / width)
        e = eff[:, cols]
        var1 = (own_m + 1.0) + e * (2.0 * gram + e * own_o)
        inv = lax.rsqrt(var1)
        q = inv * scale / (1.0 + jnp.exp(margin - 2.0 * (var1 * inv)))
        w = q * e
        w2 = split(w)
        part = dot3(w2, o2, ((1,), (0,))) + jnp.sum(q, axis=1, keepdims=True) * psi_m
        part = part.reshape(n_out, SEL_M, width)
        if chunks == 1:
            mpart[...] = part
        else:
            @pl.when(ch == 0)
            def _():
                mpart[...] = part

            @pl.when(ch > 0)
            def _():
                mpart[...] += part
        c2 = split(w * e)
        dn0 = (((0,), (0,)), ((), ()))
        colsum = (lax.dot_general(c2[0], ones_m, dn0, preferred_element_type=F32)
                  + lax.dot_general(c2[1], ones_m, dn0, preferred_element_type=F32))[:, 0:1]
        a = dot3(w2, m2, ((0,), (0,))) + colsum * psi_o
        a = a.reshape(per, SEL_O, width)
        for b in range(per):
            adj[b % 2, ch * (per // 2) + b // 2] = a[b]
        return 0

    if chunks == 1:
        compute(0, 0)
    else:
        lax.fori_loop(0, chunks, compute, 0)

    def sib_copy(d):
        zz = to_z(d)
        return pltpu.make_async_remote_copy(
            adj.at[1 - c, zz], rs.at[zz], bs_s.at[zz], bs_r.at[zz],
            device_id={"mon": sib}, device_id_type=MESH)

    def z_copy(d):
        zz = to_z(d)
        return pltpu.make_async_remote_copy(
            adj.at[c, zz], rz.at[z], bz_s.at[d], bz_r.at[z],
            device_id={"mon": 2 * zz + c}, device_id_type=MESH)

    def z_recv(d):
        zz = from_z(d)
        return pltpu.make_async_remote_copy(
            adj.at[c, zz], rz.at[zz], bz_s.at[d], bz_r.at[zz],
            device_id={"mon": 2 * zz + c}, device_id_type=MESH)

    def b_copy(d):
        p = to_out(d + 1)
        return pltpu.make_async_remote_copy(
            mpart.at[p], rm.at[j], bm_s.at[d], bm_r.at[j],
            device_id={"out": p}, device_id_type=MESH)

    def b_recv(d):
        s = from_out(d + 1)
        return pltpu.make_async_remote_copy(
            mpart.at[s], rm.at[s], bm_s.at[d], bm_r.at[s],
            device_id={"out": s}, device_id_type=MESH)

    loop(nz, lambda d: sib_copy((d + 1) % nz if isinstance(d, int) else lax.rem(d + 1, nz)).start())
    loop(n_out - 1, lambda d: b_copy(d).start())

    def pass_z(d):
        zz = to_z(d + 1)
        sib_copy(d + 1).wait_recv()
        adj[c, zz] = adj[c, zz] + rs[zz]
        z_copy(d + 1).start()

    loop(nz - 1, pass_z)
    sib_copy(0).wait_recv()
    rz[z] = adj[c, z] + rs[z]

    loop(nz - 1, lambda d: z_recv(d + 1).wait_recv())
    if nz <= 8:
        tot = rz[z]
        for d in range(1, nz):
            tot = tot + rz[from_z(d)]
    else:
        tot = lax.fori_loop(1, nz, lambda d, t: t + rz[from_z(d)], rz[z])
    t0 = tot.astype(BF16)
    r1 = tot - t0.astype(F32)
    t1 = r1.astype(BF16)
    t2 = (r1 - t1.astype(F32)).astype(BF16)
    st = selt[...].astype(BF16)
    dn0 = (((0,), (0,)), ((), ()))
    put = functools.partial(lax.dot_general, dimension_numbers=dn0, preferred_element_type=F32)
    res = put(st, t0) + (put(st, t1) + put(st, t2)) + mpart[j]
    for d in range(n_out - 1):
        b_recv(d).wait_recv()
        res = res + rm[from_out(d + 1)]
    out_ref[...] = res

    loop(nz - 1, lambda d: copy_o(d).wait_send())
    loop(n_out - 1, lambda d: copy_m(d).wait_send())
    copy_s().wait_send()
    loop(nz - 1, lambda d: relay(d).wait_send())
    loop(nz, lambda d: sib_copy(d).wait_send())
    loop(nz - 1, lambda d: z_copy(d + 1).wait_send())
    loop(n_out - 1, lambda d: b_copy(d).wait_send())


def body(n_mon, n_out, psi, lodf, block_map, margin, monitored, outages):
    width = psi.shape[1]
    mon_count = monitored.shape[0]
    out_count = outages.shape[0]
    nz = n_mon // 2
    total_out = out_count * n_out
    vm = pl.BlockSpec(memory_space=pltpu.VMEM)
    dma = pltpu.SemaphoreType.DMA
    return pl.pallas_call(
        functools.partial(kernel, n_mon, n_out, 2.0 / total_out),
        out_shape=jax.ShapeDtypeStruct(psi.shape, F32),
        in_specs=[pl.BlockSpec(memory_space=pl.ANY)] * 6,
        out_specs=vm,
        scratch_shapes=[
            pltpu.VMEM(lodf.shape, F32),
            pltpu.SMEM(block_map.shape, jnp.int32),
            pltpu.VMEM((1, mon_count), F32),
            pltpu.VMEM((1, mon_count), jnp.int32),
            pltpu.SMEM(outages.shape, jnp.int32),
            pltpu.VMEM(psi.shape, F32),
            pltpu.VMEM((n_out, BR_DEV, width), F32),
            pltpu.VMEM((n_mon, SEL_O, width), F32),
            pltpu.VMEM((SEL_O, width), F32),
            pltpu.VMEM((SEL_O, BR_DEV), F32),
            pltpu.VMEM((mon_count, out_count), F32),
            pltpu.VMEM((mon_count, 1), F32),
            pltpu.VMEM((n_out, BR_DEV, width), F32),
            pltpu.VMEM((2, nz, SEL_O, width), F32),
            pltpu.VMEM((n_out, BR_DEV, width), F32),
            pltpu.VMEM((nz, SEL_O, width), F32),
            pltpu.VMEM((nz, SEL_O, width), F32),
            dma((6,)), dma((n_out - 1,)), dma((n_out,)), dma((nz,)), dma((n_mon,)),
            dma(()), dma((nz,)), dma((n_out - 1,)), dma((n_out,)),
            dma((nz,)), dma((nz,)), dma((nz,)), dma((nz,)),
        ],
        compiler_params=pltpu.CompilerParams(
            collective_id=0, has_side_effects=True, vmem_limit_bytes=40 << 20),
        name="flow_variance_grad",
    )(*[pltpu.with_memory_space_constraint(x, pltpu.HBM) for x in (psi, lodf, block_map, margin.reshape(1, -1), monitored.reshape(1, -1), outages)])


def solution(mesh):
    in_specs = (
        P(("grp", "mon", "out"), None),
        P(("grp", "mon"), "out"),
        P(("grp", "mon"), "out"),
        P(("grp", "mon")),
        P(("grp", "mon")),
        P(("grp", "out")),
    )
    out_specs = P(("grp", "mon", "out"), None)
    fn = functools.partial(body, mesh.shape["mon"], mesh.shape["out"])
    return jax.shard_map(fn, mesh=mesh, in_specs=in_specs, out_specs=out_specs, check_vma=False)
```

```python
import functools

import jax
import jax.numpy as jnp
from jax import lax
from jax.experimental import pallas as pl
from jax.experimental.pallas import tpu as pltpu
from jax.sharding import PartitionSpec as P

BR_DEV = 64
SEL_M = 64
SEL_O = 32
LB = 128
OC = 256
MESH = pl.DeviceIdType.MESH
F32 = jnp.float32
BF16 = jnp.bfloat16


def split(a):
    hi = a.astype(BF16)
    return hi, (a - hi.astype(F32)).astype(BF16)


def dot3(a, b, dims):
    dn = (dims, ((), ()))
    dot = functools.partial(lax.dot_general, dimension_numbers=dn, preferred_element_type=F32)
    return dot(a[0], b[0]) + (dot(a[0], b[1]) + dot(a[1], b[0]))


def kernel(n_mon, n_out, scale,
           psi_hbm, lodf_hbm, map_hbm, margin_hbm, mon_hbm, outs_hbm,
           out_ref,
           lodf_ref, map_ref, margin_ref, mon_ref, outs_ref,
           pv, pm, po, sel, selt, eff, marg, mh, ml, own, mpart, adj, rm, rs, rz,
           loc_sem, sm_s, sm_r, so_s, so_r, fw_s, rl_s, bm_s, bm_r, bs_s, bs_r, bz_s, bz_r):
    nz = n_mon // 2
    i = lax.axis_index("mon")
    j = lax.axis_index("out")
    z = i // 2
    c = lax.rem(i, 2)
    sib = i + 1 - 2 * c
    width = pm.shape[2]
    mon_count = n_out * SEL_M
    out_count = n_mon * SEL_O
    per = OC // SEL_O
    chunks = out_count // OC

    def to_out(d):
        return lax.rem(j + d, n_out)

    def from_out(d):
        return lax.rem(j + n_out - d, n_out)

    def to_z(d):
        return lax.rem(z + d, nz)

    def from_z(d):
        return lax.rem(z + nz - d, nz)

    def z_at(d):
        if nz != 4:
            return from_z(d + 1)
        mid = (lax.rem(z, 3) + 1) // 2
        near = (1 - mid) * (1 + z // 3) + mid * 3 * (z - 1)
        if d == 0:
            return near
        if d == 1:
            return (1 - mid) * (2 - z // 3) + mid * (3 - z)
        return (1 - mid) * (3 - z) + mid * (3 - near)

    def loop(count, f):
        if count <= 8:
            for d in range(count):
                f(d)
        else:
            lax.fori_loop(0, count, lambda d, x: (f(d), x)[1], 0)

    loads = [pltpu.make_async_copy(a, b, loc_sem.at[k]) for k, (a, b) in enumerate([
        (outs_hbm, outs_ref), (psi_hbm, pv), (mon_hbm, mon_ref),
        (margin_hbm, margin_ref), (map_hbm, map_ref), (lodf_hbm, lodf_ref)])]
    barrier = pltpu.get_barrier_semaphore()

    def sig_out(d):
        pl.semaphore_signal(barrier, inc=1, device_id={"out": to_out(d + 1)}, device_id_type=MESH)

    def sig_z(d):
        pl.semaphore_signal(barrier, inc=1, device_id={"mon": 2 * to_z(d + 1) + c}, device_id_type=MESH)

    loop(nz - 1, sig_z)
    loop(n_out - 1, sig_out)
    pl.semaphore_signal(barrier, inc=1, device_id={"mon": sib}, device_id_type=MESH)
    for load in loads:
        load.start()
    loads[0].wait()
    loads[1].wait()
    for k in range(SEL_O):
        row = lax.rem(outs_ref[i * SEL_O + k], BR_DEV)
        sel[pl.ds(k, 1), :] = pv[pl.ds(row, 1), :]
    pl.semaphore_wait(barrier, n_out - 1 + nz - 1 + 1)

    def copy_m(d):
        return pltpu.make_async_remote_copy(
            pv, pm.at[j], sm_s.at[d], sm_r.at[j],
            device_id={"out": to_out(d + 1)}, device_id_type=MESH)

    def recv_m(d):
        s = from_out(d + 1)
        return pltpu.make_async_remote_copy(
            pv, pm.at[s], sm_s.at[d], sm_r.at[s],
            device_id={"out": to_out(d + 1)}, device_id_type=MESH)

    def copy_o(d):
        return pltpu.make_async_remote_copy(
            sel, po.at[i], so_s.at[d], so_r.at[i],
            device_id={"mon": 2 * to_z(d + 1) + c}, device_id_type=MESH)

    def copy_s():
        return pltpu.make_async_remote_copy(
            sel, po.at[i], fw_s, so_r.at[i],
            device_id={"mon": sib}, device_id_type=MESH)

    def from_slot(slot):
        return pltpu.make_async_remote_copy(
            sel, po.at[slot], fw_s, so_r.at[slot],
            device_id={"mon": sib}, device_id_type=MESH)

    def relay(d):
        slot = 2 * z_at(d) + c
        return pltpu.make_async_remote_copy(
            po.at[slot], po.at[slot], rl_s.at[d], so_r.at[slot],
            device_id={"mon": sib}, device_id_type=MESH)

    loop(nz - 1, lambda d: copy_o(d).start())
    loop(n_out - 1, lambda d: copy_m(d).start())
    copy_s().start()
    po[i] = sel[...]
    pm[j] = pv[...]

    lane = lax.broadcasted_iota(jnp.int32, (1, BR_DEV), 1)
    for k in range(SEL_O):
        row = lax.rem(outs_ref[i * SEL_O + k], BR_DEV)
        selt[pl.ds(k, 1), :] = (lane == row).astype(F32)
    for load in loads[2:]:
        load.wait()
    col = lax.broadcasted_iota(jnp.int32, (1, mon_count), 1)
    place = col // SEL_M * BR_DEV + lax.rem(mon_ref[...], BR_DEV)
    hit = lax.broadcasted_iota(jnp.int32, (mon_count, mon_count), 0) == place
    marg[...] = jnp.sum(jnp.where(hit, margin_ref[...], 0.0), axis=1, keepdims=True)
    perm = hit.astype(BF16)

    def lay(ch, _):
        if chunks == 1:
            cols = slice(0, OC)
        else:
            cols = pl.ds(pl.multiple_of(ch * OC, OC), OC)
        lf = lodf_ref[:, cols]
        parts = []
        for a in range(mon_count // LB):
            parts.append(jnp.concatenate(
                [lf[a * LB:(a + 1) * LB, b * LB:(b + 1) * LB] * map_ref[a, ch * (OC // LB) + b].astype(F32)
                 for b in range(OC // LB)], axis=1))
        e = jnp.concatenate(parts, axis=0)
        e0 = e.astype(BF16)
        r1 = e - e0.astype(F32)
        e1 = r1.astype(BF16)
        e2 = (r1 - e1.astype(F32)).astype(BF16)
        dot = functools.partial(jnp.dot, preferred_element_type=F32)
        eff[:, cols] = dot(perm, e0) + (dot(perm, e1) + dot(perm, e2))
        return 0

    if chunks == 1:
        lay(0, 0)
    else:
        lax.fori_loop(0, chunks, lay, 0)

    def take_z(d):
        slot = 2 * z_at(d) + c
        from_slot(slot).wait_recv()
        relay(d).start()

    def prep(s):
        block = pm[s]
        hi, lo = split(block)
        rows = pl.ds(pl.multiple_of(s * SEL_M, SEL_M), SEL_M)
        mh[rows, :] = hi
        ml[rows, :] = lo
        own[rows, :] = jnp.sum(block * block, axis=1, keepdims=True) * (1.0 / width)

    prep(j)
    if nz <= 4:
        for d in range(max(nz, n_out) - 1):
            if d < nz - 1:
                take_z(d)
            if d < n_out - 1:
                recv_m(d).wait_recv()
                prep(from_out(d + 1))
    else:
        loop(nz - 1, take_z)
        for d in range(n_out - 1):
            recv_m(d).wait_recv()
            prep(from_out(d + 1))
    from_slot(sib).wait_recv()
    loop(nz - 1, lambda d: from_slot(2 * z_at(d) + 1 - c).wait_recv())

    psi_m = pm[...].reshape(mon_count, width)
    m2 = (mh[...], ml[...])
    own_m = own[...]
    margin = marg[...]
    ones_o = jnp.ones((8, width), BF16)
    ones_m = jnp.ones((mon_count, 128), BF16)

    def compute(ch, _):
        if chunks == 1:
            cols = slice(0, OC)
            rows = slice(0, per)
        else:
            cols = pl.ds(pl.multiple_of(ch * OC, OC), OC)
            rows = pl.ds(ch * per, per)
        psi_o = po[rows].reshape(OC, width)
        o2 = split(psi_o)
        gram = dot3(m2, o2, ((1,), (1,))) * (1.0 / width)
        s2 = split(psi_o * psi_o)
        dn = (((1,), (1,)), ((), ()))
        own_o = (lax.dot_general(ones_o, s2[0], dn, preferred_element_type=F32)
                 + lax.dot_general(ones_o, s2[1], dn, preferred_element_type=F32))[0:1] * (1.0 / width)
        e = eff[:, cols]
        var1 = (own_m + 1.0) + e * (2.0 * gram + e * own_o)
        inv = lax.rsqrt(var1)
        q = inv * scale / (1.0 + jnp.exp(margin - 2.0 * (var1 * inv)))
        w = q * e
        w2 = split(w)
        c2 = split(w * e)
        dn0 = (((0,), (0,)), ((), ()))
        colsum = (lax.dot_general(c2[0], ones_m, dn0, preferred_element_type=F32)
                  + lax.dot_general(c2[1], ones_m, dn0, preferred_element_type=F32))[:, 0:1]
        a = dot3(w2, m2, ((0,), (0,))) + colsum * psi_o
        a = a.reshape(per, SEL_O, width)
        for b in range(per):
            adj[b % 2, ch * (per // 2) + b // 2] = a[b]
        return q, w2, o2

    def rows_part(ch, q, w2, o2):
        part = dot3(w2, o2, ((1,), (0,))) + jnp.sum(q, axis=1, keepdims=True) * psi_m
        part = part.reshape(n_out, SEL_M, width)
        if chunks == 1:
            mpart[...] = part
        else:
            @pl.when(ch == 0)
            def _():
                mpart[...] = part

            @pl.when(ch > 0)
            def _():
                mpart[...] += part

    def sib_copy(d):
        zz = to_z(d)
        return pltpu.make_async_remote_copy(
            adj.at[1 - c, zz], rs.at[zz], bs_s.at[zz], bs_r.at[zz],
            device_id={"mon": sib}, device_id_type=MESH)

    def z_copy(d):
        zz = to_z(d)
        return pltpu.make_async_remote_copy(
            adj.at[c, zz], rz.at[z], bz_s.at[d], bz_r.at[z],
            device_id={"mon": 2 * zz + c}, device_id_type=MESH)

    def z_recv(d):
        zz = from_z(d)
        return pltpu.make_async_remote_copy(
            adj.at[c, zz], rz.at[zz], bz_s.at[d], bz_r.at[zz],
            device_id={"mon": 2 * zz + c}, device_id_type=MESH)

    def b_copy(d):
        p = to_out(d + 1)
        return pltpu.make_async_remote_copy(
            mpart.at[p], rm.at[j], bm_s.at[d], bm_r.at[j],
            device_id={"out": p}, device_id_type=MESH)

    def b_recv(d):
        s = from_out(d + 1)
        return pltpu.make_async_remote_copy(
            mpart.at[s], rm.at[s], bm_s.at[d], bm_r.at[s],
            device_id={"out": s}, device_id_type=MESH)

    if chunks == 1:
        mid = compute(0, 0)
        for d in range(nz):
            sib_copy((d + 1) % nz).start()
        rows_part(0, *mid)
    else:
        def chunk(ch, _):
            rows_part(ch, *compute(ch, 0))
            return 0

        lax.fori_loop(0, chunks, chunk, 0)
        loop(nz, lambda d: sib_copy(lax.rem(d + 1, nz)).start())
    loop(n_out - 1, lambda d: b_copy(d).start())

    def pass_z(d):
        zz = to_z(d + 1)
        sib_copy(d + 1).wait_recv()
        adj[c, zz] = adj[c, zz] + rs[zz]
        z_copy(d + 1).start()

    loop(nz - 1, pass_z)
    sib_copy(0).wait_recv()
    rz[z] = adj[c, z] + rs[z]

    loop(nz - 1, lambda d: z_recv(d + 1).wait_recv())
    if nz <= 8:
        tot = rz[z]
        for d in range(1, nz):
            tot = tot + rz[from_z(d)]
    else:
        tot = lax.fori_loop(1, nz, lambda d, t: t + rz[from_z(d)], rz[z])
    t0 = tot.astype(BF16)
    r1 = tot - t0.astype(F32)
    t1 = r1.astype(BF16)
    t2 = (r1 - t1.astype(F32)).astype(BF16)
    st = selt[...].astype(BF16)
    dn0 = (((0,), (0,)), ((), ()))
    put = functools.partial(lax.dot_general, dimension_numbers=dn0, preferred_element_type=F32)
    res = put(st, t0) + (put(st, t1) + put(st, t2)) + mpart[j]
    for d in range(n_out - 1):
        b_recv(d).wait_recv()
        res = res + rm[from_out(d + 1)]
    out_ref[...] = res

    loop(nz - 1, lambda d: copy_o(d).wait_send())
    loop(n_out - 1, lambda d: copy_m(d).wait_send())
    copy_s().wait_send()
    loop(nz - 1, lambda d: relay(d).wait_send())
    loop(nz, lambda d: sib_copy(d).wait_send())
    loop(nz - 1, lambda d: z_copy(d + 1).wait_send())
    loop(n_out - 1, lambda d: b_copy(d).wait_send())


def body(n_mon, n_out, psi, lodf, block_map, margin, monitored, outages):
    width = psi.shape[1]
    mon_count = monitored.shape[0]
    out_count = outages.shape[0]
    nz = n_mon // 2
    total_out = out_count * n_out
    vm = pl.BlockSpec(memory_space=pltpu.VMEM)
    dma = pltpu.SemaphoreType.DMA
    return pl.pallas_call(
        functools.partial(kernel, n_mon, n_out, 2.0 / total_out),
        out_shape=jax.ShapeDtypeStruct(psi.shape, F32),
        in_specs=[pl.BlockSpec(memory_space=pl.ANY)] * 6,
        out_specs=vm,
        scratch_shapes=[
            pltpu.VMEM(lodf.shape, F32),
            pltpu.SMEM(block_map.shape, jnp.int32),
            pltpu.VMEM((1, mon_count), F32),
            pltpu.VMEM((1, mon_count), jnp.int32),
            pltpu.SMEM(outages.shape, jnp.int32),
            pltpu.VMEM(psi.shape, F32),
            pltpu.VMEM((n_out, BR_DEV, width), F32),
            pltpu.VMEM((n_mon, SEL_O, width), F32),
            pltpu.VMEM((SEL_O, width), F32),
            pltpu.VMEM((SEL_O, BR_DEV), F32),
            pltpu.VMEM((mon_count, out_count), F32),
            pltpu.VMEM((mon_count, 1), F32),
            pltpu.VMEM((mon_count, width), BF16),
            pltpu.VMEM((mon_count, width), BF16),
            pltpu.VMEM((mon_count, 1), F32),
            pltpu.VMEM((n_out, BR_DEV, width), F32),
            pltpu.VMEM((2, nz, SEL_O, width), F32),
            pltpu.VMEM((n_out, BR_DEV, width), F32),
            pltpu.VMEM((nz, SEL_O, width), F32),
            pltpu.VMEM((nz, SEL_O, width), F32),
            dma((6,)), dma((n_out - 1,)), dma((n_out,)), dma((nz,)), dma((n_mon,)),
            dma(()), dma((nz,)), dma((n_out - 1,)), dma((n_out,)),
            dma((nz,)), dma((nz,)), dma((nz,)), dma((nz,)),
        ],
        compiler_params=pltpu.CompilerParams(
            collective_id=0, has_side_effects=True, vmem_limit_bytes=40 << 20),
        name="flow_variance_grad",
    )(*[pltpu.with_memory_space_constraint(x, pltpu.HBM) for x in (psi, lodf, block_map, margin.reshape(1, -1), monitored.reshape(1, -1), outages)])


def solution(mesh):
    in_specs = (
        P(("grp", "mon", "out"), None),
        P(("grp", "mon"), "out"),
        P(("grp", "mon"), "out"),
        P(("grp", "mon")),
        P(("grp", "mon")),
        P(("grp", "out")),
    )
    out_specs = P(("grp", "mon", "out"), None)
    fn = functools.partial(body, mesh.shape["mon"], mesh.shape["out"])
    return jax.shard_map(fn, mesh=mesh, in_specs=in_specs, out_specs=out_specs, check_vma=False)
```

```python
import functools

import jax
import jax.numpy as jnp
from jax import lax
from jax.experimental import pallas as pl
from jax.experimental.pallas import tpu as pltpu
from jax.sharding import PartitionSpec as P

BR_DEV = 64
SEL_M = 64
SEL_O = 32
LB = 128
OC = 256
MESH = pl.DeviceIdType.MESH
F32 = jnp.float32
BF16 = jnp.bfloat16


def split(a):
    hi = a.astype(BF16)
    return hi, (a - hi.astype(F32)).astype(BF16)


def dot3(a, b, dims):
    dn = (dims, ((), ()))
    dot = functools.partial(lax.dot_general, dimension_numbers=dn, preferred_element_type=F32)
    return dot(a[0], b[0]) + (dot(a[0], b[1]) + dot(a[1], b[0]))


def kernel(n_mon, n_out, scale,
           psi_hbm, lodf_hbm, map_hbm, margin_hbm, mon_hbm, outs_hbm,
           out_ref,
           lodf_ref, map_ref, margin_ref, mon_ref, outs_ref,
           pv, pm, po, sel, selt, eff, efft, marg, mpart, adj, rm, rs, rz,
           loc_sem, sm_s, sm_r, so_s, so_r, fw_s, rl_s, bm_s, bm_r, bs_s, bs_r, bz_s, bz_r):
    nz = n_mon // 2
    i = lax.axis_index("mon")
    j = lax.axis_index("out")
    z = i // 2
    c = lax.rem(i, 2)
    sib = i + 1 - 2 * c
    width = pm.shape[2]
    mon_count = n_out * SEL_M
    out_count = n_mon * SEL_O
    per = OC // SEL_O
    chunks = out_count // OC

    def to_out(d):
        return lax.rem(j + d, n_out)

    def from_out(d):
        return lax.rem(j + n_out - d, n_out)

    def to_z(d):
        return lax.rem(z + d, nz)

    def from_z(d):
        return lax.rem(z + nz - d, nz)

    def z_at(d):
        return from_z(d + 1)
        mid = (lax.rem(z, 3) + 1) // 2
        near = (1 - mid) * (1 + z // 3) + mid * 3 * (z - 1)
        if d == 0:
            return near
        if d == 1:
            return (1 - mid) * (2 - z // 3) + mid * (3 - z)
        return (1 - mid) * (3 - z) + mid * (3 - near)

    def loop(count, f):
        if count <= 8:
            for d in range(count):
                f(d)
        else:
            lax.fori_loop(0, count, lambda d, x: (f(d), x)[1], 0)

    loads = [pltpu.make_async_copy(a, b, loc_sem.at[k]) for k, (a, b) in enumerate([
        (outs_hbm, outs_ref), (psi_hbm, pv), (mon_hbm, mon_ref),
        (margin_hbm, margin_ref), (map_hbm, map_ref), (lodf_hbm, lodf_ref)])]
    barrier = pltpu.get_barrier_semaphore()

    def sig_out(d):
        pl.semaphore_signal(barrier, inc=1, device_id={"out": to_out(d + 1)}, device_id_type=MESH)

    def sig_z(d):
        pl.semaphore_signal(barrier, inc=1, device_id={"mon": 2 * to_z(d + 1) + c}, device_id_type=MESH)

    loop(nz - 1, sig_z)
    loop(n_out - 1, sig_out)
    pl.semaphore_signal(barrier, inc=1, device_id={"mon": sib}, device_id_type=MESH)
    for load in loads:
        load.start()
    loads[0].wait()
    loads[1].wait()
    for k in range(SEL_O):
        row = lax.rem(outs_ref[i * SEL_O + k], BR_DEV)
        sel[pl.ds(k, 1), :] = pv[pl.ds(row, 1), :]
    pl.semaphore_wait(barrier, n_out - 1 + nz - 1 + 1)

    def copy_m(d):
        return pltpu.make_async_remote_copy(
            pv, pm.at[j], sm_s.at[d], sm_r.at[j],
            device_id={"out": to_out(d + 1)}, device_id_type=MESH)

    def recv_m(d):
        s = from_out(d + 1)
        return pltpu.make_async_remote_copy(
            pv, pm.at[s], sm_s.at[d], sm_r.at[s],
            device_id={"out": to_out(d + 1)}, device_id_type=MESH)

    def copy_o(d):
        return pltpu.make_async_remote_copy(
            sel, po.at[i], so_s.at[d], so_r.at[i],
            device_id={"mon": 2 * to_z(d + 1) + c}, device_id_type=MESH)

    def copy_s():
        return pltpu.make_async_remote_copy(
            sel, po.at[i], fw_s, so_r.at[i],
            device_id={"mon": sib}, device_id_type=MESH)

    def from_slot(slot):
        return pltpu.make_async_remote_copy(
            sel, po.at[slot], fw_s, so_r.at[slot],
            device_id={"mon": sib}, device_id_type=MESH)

    def relay(d):
        slot = 2 * z_at(d) + c
        return pltpu.make_async_remote_copy(
            po.at[slot], po.at[slot], rl_s.at[d], so_r.at[slot],
            device_id={"mon": sib}, device_id_type=MESH)

    loop(nz - 1, lambda d: copy_o(d).start())
    loop(n_out - 1, lambda d: copy_m(d).start())
    copy_s().start()
    po[i] = sel[...]
    pm[j] = pv[...]

    lane = lax.broadcasted_iota(jnp.int32, (1, BR_DEV), 1)
    for k in range(SEL_O):
        row = lax.rem(outs_ref[i * SEL_O + k], BR_DEV)
        selt[pl.ds(k, 1), :] = (lane == row).astype(F32)
    for load in loads[2:]:
        load.wait()
    col = lax.broadcasted_iota(jnp.int32, (1, mon_count), 1)
    place = col // SEL_M * BR_DEV + lax.rem(mon_ref[...], BR_DEV)
    hit = lax.broadcasted_iota(jnp.int32, (mon_count, mon_count), 0) == place
    marg[...] = jnp.sum(jnp.where(hit, margin_ref[...], 0.0), axis=1, keepdims=True)
    perm = hit.astype(BF16)

    def lay(ch, _):
        if chunks == 1:
            cols = slice(0, OC)
        else:
            cols = pl.ds(pl.multiple_of(ch * OC, OC), OC)
        lf = lodf_ref[:, cols]
        parts = []
        for a in range(mon_count // LB):
            parts.append(jnp.concatenate(
                [lf[a * LB:(a + 1) * LB, b * LB:(b + 1) * LB] * map_ref[a, ch * (OC // LB) + b].astype(F32)
                 for b in range(OC // LB)], axis=1))
        e = jnp.concatenate(parts, axis=0)
        e0 = e.astype(BF16)
        r1 = e - e0.astype(F32)
        e1 = r1.astype(BF16)
        e2 = (r1 - e1.astype(F32)).astype(BF16)
        dot = functools.partial(jnp.dot, preferred_element_type=F32)
        laid = dot(perm, e0) + (dot(perm, e1) + dot(perm, e2))
        eff[:, cols] = laid
        efft[cols, :] = laid.T
        return 0

    if chunks == 1:
        lay(0, 0)
    else:
        lax.fori_loop(0, chunks, lay, 0)

    def take_z(d):
        slot = 2 * z_at(d) + c
        from_slot(slot).wait_recv()
        relay(d).start()

    loop(nz - 1, take_z)
    loop(n_out - 1, lambda d: recv_m(d).wait_recv())
    from_slot(sib).wait_recv()
    loop(nz - 1, lambda d: from_slot(2 * z_at(d) + 1 - c).wait_recv())

    psi_m = pm[...].reshape(mon_count, width)
    m2 = split(psi_m)
    own_m = jnp.sum(psi_m * psi_m, axis=1, keepdims=True) * (1.0 / width)
    margin = marg[...]
    ones_o = jnp.ones((8, width), BF16)

    def compute(ch, _):
        if chunks == 1:
            cols = slice(0, OC)
            rows = slice(0, per)
        else:
            cols = pl.ds(pl.multiple_of(ch * OC, OC), OC)
            rows = pl.ds(ch * per, per)
        psi_o = po[rows].reshape(OC, width)
        o2 = split(psi_o)
        gram = dot3(m2, o2, ((1,), (1,))) * (1.0 / width)
        s2 = split(psi_o * psi_o)
        dn = (((1,), (1,)), ((), ()))
        own_o = (lax.dot_general(ones_o, s2[0], dn, preferred_element_type=F32)
                 + lax.dot_general(ones_o, s2[1], dn, preferred_element_type=F32))[0:1] * (1.0 / width)
        e = eff[:, cols]
        var1 = (own_m + 1.0) + e * (2.0 * gram + e * own_o)
        inv = lax.rsqrt(var1)
        q = inv * scale / (1.0 + jnp.exp(margin - 2.0 * (var1 * inv)))
        w = q * e
        w2 = split(w)
        wt = w.T
        colsum = jnp.sum(wt * efft[cols, :], axis=1, keepdims=True)
        a = dot3(split(wt), m2, ((1,), (0,))) + colsum * psi_o
        a = a.reshape(per, SEL_O, width)
        for b in range(per):
            adj[b % 2, ch * (per // 2) + b // 2] = a[b]
        return q, w2, o2

    def rows_part(ch, q, w2, o2):
        part = dot3(w2, o2, ((1,), (0,))) + jnp.sum(q, axis=1, keepdims=True) * psi_m
        part = part.reshape(n_out, SEL_M, width)
        if chunks == 1:
            mpart[...] = part
        else:
            @pl.when(ch == 0)
            def _():
                mpart[...] = part

            @pl.when(ch > 0)
            def _():
                mpart[...] += part

    def sib_copy(d):
        zz = to_z(d)
        return pltpu.make_async_remote_copy(
            adj.at[1 - c, zz], rs.at[zz], bs_s.at[zz], bs_r.at[zz],
            device_id={"mon": sib}, device_id_type=MESH)

    def z_copy(d):
        zz = to_z(d)
        return pltpu.make_async_remote_copy(
            adj.at[c, zz], rz.at[z], bz_s.at[d], bz_r.at[z],
            device_id={"mon": 2 * zz + c}, device_id_type=MESH)

    def z_recv(d):
        zz = from_z(d)
        return pltpu.make_async_remote_copy(
            adj.at[c, zz], rz.at[zz], bz_s.at[d], bz_r.at[zz],
            device_id={"mon": 2 * zz + c}, device_id_type=MESH)

    def b_copy(d):
        p = to_out(d + 1)
        return pltpu.make_async_remote_copy(
            mpart.at[p], rm.at[j], bm_s.at[d], bm_r.at[j],
            device_id={"out": p}, device_id_type=MESH)

    def b_recv(d):
        s = from_out(d + 1)
        return pltpu.make_async_remote_copy(
            mpart.at[s], rm.at[s], bm_s.at[d], bm_r.at[s],
            device_id={"out": s}, device_id_type=MESH)

    if chunks == 1:
        mid = compute(0, 0)
        for d in range(nz):
            sib_copy((d + 1) % nz).start()
        rows_part(0, *mid)
    else:
        def chunk(ch, _):
            rows_part(ch, *compute(ch, 0))
            return 0

        lax.fori_loop(0, chunks, chunk, 0)
        loop(nz, lambda d: sib_copy(lax.rem(d + 1, nz)).start())
    loop(n_out - 1, lambda d: b_copy(d).start())

    def pass_z(d):
        zz = to_z(d + 1)
        sib_copy(d + 1).wait_recv()
        adj[c, zz] = adj[c, zz] + rs[zz]
        z_copy(d + 1).start()

    loop(nz - 1, pass_z)
    sib_copy(0).wait_recv()
    rz[z] = adj[c, z] + rs[z]

    loop(nz - 1, lambda d: z_recv(d + 1).wait_recv())
    if nz <= 8:
        tot = rz[z]
        for d in range(1, nz):
            tot = tot + rz[from_z(d)]
    else:
        tot = lax.fori_loop(1, nz, lambda d, t: t + rz[from_z(d)], rz[z])
    t0 = tot.astype(BF16)
    r1 = tot - t0.astype(F32)
    t1 = r1.astype(BF16)
    t2 = (r1 - t1.astype(F32)).astype(BF16)
    st = selt[...].astype(BF16)
    dn0 = (((0,), (0,)), ((), ()))
    put = functools.partial(lax.dot_general, dimension_numbers=dn0, preferred_element_type=F32)
    res = put(st, t0) + (put(st, t1) + put(st, t2)) + mpart[j]
    for d in range(n_out - 1):
        b_recv(d).wait_recv()
        res = res + rm[from_out(d + 1)]
    out_ref[...] = res

    loop(nz - 1, lambda d: copy_o(d).wait_send())
    loop(n_out - 1, lambda d: copy_m(d).wait_send())
    copy_s().wait_send()
    loop(nz - 1, lambda d: relay(d).wait_send())
    loop(nz, lambda d: sib_copy(d).wait_send())
    loop(nz - 1, lambda d: z_copy(d + 1).wait_send())
    loop(n_out - 1, lambda d: b_copy(d).wait_send())


def body(n_mon, n_out, psi, lodf, block_map, margin, monitored, outages):
    width = psi.shape[1]
    mon_count = monitored.shape[0]
    out_count = outages.shape[0]
    nz = n_mon // 2
    total_out = out_count * n_out
    vm = pl.BlockSpec(memory_space=pltpu.VMEM)
    dma = pltpu.SemaphoreType.DMA
    return pl.pallas_call(
        functools.partial(kernel, n_mon, n_out, 2.0 / total_out),
        out_shape=jax.ShapeDtypeStruct(psi.shape, F32),
        in_specs=[pl.BlockSpec(memory_space=pl.ANY)] * 6,
        out_specs=vm,
        scratch_shapes=[
            pltpu.VMEM(lodf.shape, F32),
            pltpu.SMEM(block_map.shape, jnp.int32),
            pltpu.VMEM((1, mon_count), F32),
            pltpu.VMEM((1, mon_count), jnp.int32),
            pltpu.SMEM(outages.shape, jnp.int32),
            pltpu.VMEM(psi.shape, F32),
            pltpu.VMEM((n_out, BR_DEV, width), F32),
            pltpu.VMEM((n_mon, SEL_O, width), F32),
            pltpu.VMEM((SEL_O, width), F32),
            pltpu.VMEM((SEL_O, BR_DEV), F32),
            pltpu.VMEM((mon_count, out_count), F32),
            pltpu.VMEM((out_count, mon_count), F32),
            pltpu.VMEM((mon_count, 1), F32),
            pltpu.VMEM((n_out, BR_DEV, width), F32),
            pltpu.VMEM((2, nz, SEL_O, width), F32),
            pltpu.VMEM((n_out, BR_DEV, width), F32),
            pltpu.VMEM((nz, SEL_O, width), F32),
            pltpu.VMEM((nz, SEL_O, width), F32),
            dma((6,)), dma((n_out - 1,)), dma((n_out,)), dma((nz,)), dma((n_mon,)),
            dma(()), dma((nz,)), dma((n_out - 1,)), dma((n_out,)),
            dma((nz,)), dma((nz,)), dma((nz,)), dma((nz,)),
        ],
        compiler_params=pltpu.CompilerParams(
            collective_id=0, has_side_effects=True, vmem_limit_bytes=40 << 20),
        name="flow_variance_grad",
    )(*[pltpu.with_memory_space_constraint(x, pltpu.HBM) for x in (psi, lodf, block_map, margin.reshape(1, -1), monitored.reshape(1, -1), outages)])


def solution(mesh):
    in_specs = (
        P(("grp", "mon", "out"), None),
        P(("grp", "mon"), "out"),
        P(("grp", "mon"), "out"),
        P(("grp", "mon")),
        P(("grp", "mon")),
        P(("grp", "out")),
    )
    out_specs = P(("grp", "mon", "out"), None)
    fn = functools.partial(body, mesh.shape["mon"], mesh.shape["out"])
    return jax.shard_map(fn, mesh=mesh, in_specs=in_specs, out_specs=out_specs, check_vma=False)
```

```python
import functools

import jax
import jax.numpy as jnp
from jax import lax
from jax.experimental import pallas as pl
from jax.experimental.pallas import tpu as pltpu
from jax.sharding import PartitionSpec as P

BR_DEV = 64
SEL_M = 64
SEL_O = 32
LB = 128
OC = 256
MESH = pl.DeviceIdType.MESH
F32 = jnp.float32
BF16 = jnp.bfloat16


def split(a):
    hi = a.astype(BF16)
    return hi, (a - hi.astype(F32)).astype(BF16)


def dot3(a, b, dims):
    dn = (dims, ((), ()))
    dot = functools.partial(lax.dot_general, dimension_numbers=dn, preferred_element_type=F32)
    return dot(a[0], b[0]) + (dot(a[0], b[1]) + dot(a[1], b[0]))


def kernel(n_mon, n_out, scale,
           psi_hbm, lodf_hbm, map_hbm, margin_hbm, mon_hbm, outs_hbm,
           out_ref,
           lodf_ref, map_ref, margin_ref, mon_ref, outs_ref,
           pv, pm, po, sel, selt, eff, efft, marg, mh, ml, own, mpart, adj, rm, rs, rz,
           loc_sem, sm_s, sm_r, so_s, so_r, fw_s, rl_s, bm_s, bm_r, bs_s, bs_r, bz_s, bz_r):
    nz = n_mon // 2
    i = lax.axis_index("mon")
    j = lax.axis_index("out")
    z = i // 2
    c = lax.rem(i, 2)
    sib = i + 1 - 2 * c
    width = pm.shape[2]
    mon_count = n_out * SEL_M
    out_count = n_mon * SEL_O
    per = OC // SEL_O
    chunks = out_count // OC

    def to_out(d):
        return lax.rem(j + d, n_out)

    def from_out(d):
        return lax.rem(j + n_out - d, n_out)

    def to_z(d):
        return lax.rem(z + d, nz)

    def from_z(d):
        return lax.rem(z + nz - d, nz)

    def loop(count, f):
        if count <= 8:
            for d in range(count):
                f(d)
        else:
            lax.fori_loop(0, count, lambda d, x: (f(d), x)[1], 0)

    loads = [pltpu.make_async_copy(a, b, loc_sem.at[k]) for k, (a, b) in enumerate([
        (outs_hbm, outs_ref), (psi_hbm, pv), (mon_hbm, mon_ref),
        (margin_hbm, margin_ref), (map_hbm, map_ref), (lodf_hbm, lodf_ref)])]
    barrier = pltpu.get_barrier_semaphore()

    def sig_out(d):
        pl.semaphore_signal(barrier, inc=1, device_id={"out": to_out(d + 1)}, device_id_type=MESH)

    def sig_z(d):
        pl.semaphore_signal(barrier, inc=1, device_id={"mon": 2 * to_z(d + 1) + c}, device_id_type=MESH)

    loop(nz - 1, sig_z)
    loop(n_out - 1, sig_out)
    pl.semaphore_signal(barrier, inc=1, device_id={"mon": sib}, device_id_type=MESH)
    for load in loads:
        load.start()
    loads[0].wait()
    loads[1].wait()
    for k in range(SEL_O):
        row = lax.rem(outs_ref[i * SEL_O + k], BR_DEV)
        sel[pl.ds(k, 1), :] = pv[pl.ds(row, 1), :]
    pl.semaphore_wait(barrier, n_out - 1 + nz - 1 + 1)

    def copy_m(d):
        return pltpu.make_async_remote_copy(
            pv, pm.at[j], sm_s.at[d], sm_r.at[j],
            device_id={"out": to_out(d + 1)}, device_id_type=MESH)

    def recv_m(d):
        s = from_out(d + 1)
        return pltpu.make_async_remote_copy(
            pv, pm.at[s], sm_s.at[d], sm_r.at[s],
            device_id={"out": to_out(d + 1)}, device_id_type=MESH)

    def copy_o(d):
        return pltpu.make_async_remote_copy(
            sel, po.at[i], so_s.at[d], so_r.at[i],
            device_id={"mon": 2 * to_z(d + 1) + c}, device_id_type=MESH)

    def copy_s():
        return pltpu.make_async_remote_copy(
            sel, po.at[i], fw_s, so_r.at[i],
            device_id={"mon": sib}, device_id_type=MESH)

    def from_slot(slot):
        return pltpu.make_async_remote_copy(
            sel, po.at[slot], fw_s, so_r.at[slot],
            device_id={"mon": sib}, device_id_type=MESH)

    def relay(d):
        slot = 2 * from_z(d + 1) + c
        return pltpu.make_async_remote_copy(
            po.at[slot], po.at[slot], rl_s.at[d], so_r.at[slot],
            device_id={"mon": sib}, device_id_type=MESH)

    loop(nz - 1, lambda d: copy_o(d).start())
    loop(n_out - 1, lambda d: copy_m(d).start())
    copy_s().start()
    po[i] = sel[...]
    pm[j] = pv[...]

    lane = lax.broadcasted_iota(jnp.int32, (1, BR_DEV), 1)
    for k in range(SEL_O):
        row = lax.rem(outs_ref[i * SEL_O + k], BR_DEV)
        selt[pl.ds(k, 1), :] = (lane == row).astype(F32)
    for load in loads[2:]:
        load.wait()
    col = lax.broadcasted_iota(jnp.int32, (1, mon_count), 1)
    place = col // SEL_M * BR_DEV + lax.rem(mon_ref[...], BR_DEV)
    hit = lax.broadcasted_iota(jnp.int32, (mon_count, mon_count), 0) == place
    marg[...] = jnp.sum(jnp.where(hit, margin_ref[...], 0.0), axis=1, keepdims=True)
    perm = hit.astype(BF16)

    def lay(ch, _):
        if chunks == 1:
            cols = slice(0, OC)
        else:
            cols = pl.ds(pl.multiple_of(ch * OC, OC), OC)
        lf = lodf_ref[:, cols]
        parts = []
        for a in range(mon_count // LB):
            parts.append(jnp.concatenate(
                [lf[a * LB:(a + 1) * LB, b * LB:(b + 1) * LB] * map_ref[a, ch * (OC // LB) + b].astype(F32)
                 for b in range(OC // LB)], axis=1))
        e = jnp.concatenate(parts, axis=0)
        e0 = e.astype(BF16)
        r1 = e - e0.astype(F32)
        e1 = r1.astype(BF16)
        e2 = (r1 - e1.astype(F32)).astype(BF16)
        dot = functools.partial(jnp.dot, preferred_element_type=F32)
        laid = dot(perm, e0) + (dot(perm, e1) + dot(perm, e2))
        eff[:, cols] = laid
        efft[cols, :] = laid.T
        return 0

    if chunks == 1:
        lay(0, 0)
    else:
        lax.fori_loop(0, chunks, lay, 0)

    def take_z(d):
        slot = 2 * from_z(d + 1) + c
        from_slot(slot).wait_recv()
        relay(d).start()

    loop(nz - 1, take_z)
    loop(n_out - 1, lambda d: recv_m(d).wait_recv())
    block = pm[...].reshape(mon_count, width)
    hi, lo = split(block)
    mh[...] = hi
    ml[...] = lo
    own[...] = jnp.sum(block * block, axis=1, keepdims=True) * (1.0 / width)
    from_slot(sib).wait_recv()
    loop(nz - 1, lambda d: from_slot(2 * from_z(d + 1) + 1 - c).wait_recv())

    psi_m = pm[...].reshape(mon_count, width)
    m2 = (mh[...], ml[...])
    own_m = own[...]
    margin = marg[...]
    ones_o = jnp.ones((8, width), BF16)

    def compute(ch, _):
        if chunks == 1:
            cols = slice(0, OC)
            rows = slice(0, per)
        else:
            cols = pl.ds(pl.multiple_of(ch * OC, OC), OC)
            rows = pl.ds(ch * per, per)
        psi_o = po[rows].reshape(OC, width)
        o2 = split(psi_o)
        gram = dot3(m2, o2, ((1,), (1,))) * (1.0 / width)
        s2 = split(psi_o * psi_o)
        dn = (((1,), (1,)), ((), ()))
        own_o = (lax.dot_general(ones_o, s2[0], dn, preferred_element_type=F32)
                 + lax.dot_general(ones_o, s2[1], dn, preferred_element_type=F32))[0:1] * (1.0 / width)
        e = eff[:, cols]
        var1 = (own_m + 1.0) + e * (2.0 * gram + e * own_o)
        inv = lax.rsqrt(var1)
        q = inv * scale / (1.0 + jnp.exp(margin - 2.0 * (var1 * inv)))
        w = q * e
        w2 = split(w)
        wt = w.T
        colsum = jnp.sum(wt * efft[cols, :], axis=1, keepdims=True)
        a = dot3(split(wt), m2, ((1,), (0,))) + colsum * psi_o
        a = a.reshape(per, SEL_O, width)
        for b in range(per):
            adj[b % 2, ch * (per // 2) + b // 2] = a[b]
        return q, w2, o2

    def rows_part(ch, q, w2, o2):
        part = dot3(w2, o2, ((1,), (0,))) + jnp.sum(q, axis=1, keepdims=True) * psi_m
        part = part.reshape(n_out, SEL_M, width)
        if chunks == 1:
            mpart[...] = part
        else:
            @pl.when(ch == 0)
            def _():
                mpart[...] = part

            @pl.when(ch > 0)
            def _():
                mpart[...] += part

    def sib_copy(d):
        zz = to_z(d)
        return pltpu.make_async_remote_copy(
            adj.at[1 - c, zz], rs.at[zz], bs_s.at[zz], bs_r.at[zz],
            device_id={"mon": sib}, device_id_type=MESH)

    def z_copy(d):
        zz = to_z(d)
        return pltpu.make_async_remote_copy(
            adj.at[c, zz], rz.at[z], bz_s.at[d], bz_r.at[z],
            device_id={"mon": 2 * zz + c}, device_id_type=MESH)

    def z_recv(d):
        zz = from_z(d)
        return pltpu.make_async_remote_copy(
            adj.at[c, zz], rz.at[zz], bz_s.at[d], bz_r.at[zz],
            device_id={"mon": 2 * zz + c}, device_id_type=MESH)

    def b_copy(d):
        p = to_out(d + 1)
        return pltpu.make_async_remote_copy(
            mpart.at[p], rm.at[j], bm_s.at[d], bm_r.at[j],
            device_id={"out": p}, device_id_type=MESH)

    def b_recv(d):
        s = from_out(d + 1)
        return pltpu.make_async_remote_copy(
            mpart.at[s], rm.at[s], bm_s.at[d], bm_r.at[s],
            device_id={"out": s}, device_id_type=MESH)

    if chunks == 1:
        mid = compute(0, 0)
        for d in range(nz):
            sib_copy((d + 1) % nz).start()
        rows_part(0, *mid)
    else:
        def chunk(ch, _):
            rows_part(ch, *compute(ch, 0))
            return 0

        lax.fori_loop(0, chunks, chunk, 0)
        loop(nz, lambda d: sib_copy(lax.rem(d + 1, nz)).start())
    loop(n_out - 1, lambda d: b_copy(d).start())

    def pass_z(d):
        zz = to_z(d + 1)
        sib_copy(d + 1).wait_recv()
        adj[c, zz] = adj[c, zz] + rs[zz]
        z_copy(d + 1).start()

    loop(nz - 1, pass_z)
    sib_copy(0).wait_recv()
    rz[z] = adj[c, z] + rs[z]

    loop(nz - 1, lambda d: z_recv(d + 1).wait_recv())
    if nz <= 8:
        tot = rz[z]
        for d in range(1, nz):
            tot = tot + rz[from_z(d)]
    else:
        tot = lax.fori_loop(1, nz, lambda d, t: t + rz[from_z(d)], rz[z])
    t0 = tot.astype(BF16)
    r1 = tot - t0.astype(F32)
    t1 = r1.astype(BF16)
    t2 = (r1 - t1.astype(F32)).astype(BF16)
    st = selt[...].astype(BF16)
    dn0 = (((0,), (0,)), ((), ()))
    put = functools.partial(lax.dot_general, dimension_numbers=dn0, preferred_element_type=F32)
    res = put(st, t0) + (put(st, t1) + put(st, t2)) + mpart[j]
    for d in range(n_out - 1):
        b_recv(d).wait_recv()
        res = res + rm[from_out(d + 1)]
    out_ref[...] = res

    loop(nz - 1, lambda d: copy_o(d).wait_send())
    loop(n_out - 1, lambda d: copy_m(d).wait_send())
    copy_s().wait_send()
    loop(nz - 1, lambda d: relay(d).wait_send())
    loop(nz, lambda d: sib_copy(d).wait_send())
    loop(nz - 1, lambda d: z_copy(d + 1).wait_send())
    loop(n_out - 1, lambda d: b_copy(d).wait_send())


def body(n_mon, n_out, psi, lodf, block_map, margin, monitored, outages):
    width = psi.shape[1]
    mon_count = monitored.shape[0]
    out_count = outages.shape[0]
    nz = n_mon // 2
    total_out = out_count * n_out
    vm = pl.BlockSpec(memory_space=pltpu.VMEM)
    dma = pltpu.SemaphoreType.DMA
    return pl.pallas_call(
        functools.partial(kernel, n_mon, n_out, 2.0 / total_out),
        out_shape=jax.ShapeDtypeStruct(psi.shape, F32),
        in_specs=[pl.BlockSpec(memory_space=pl.ANY)] * 6,
        out_specs=vm,
        scratch_shapes=[
            pltpu.VMEM(lodf.shape, F32),
            pltpu.SMEM(block_map.shape, jnp.int32),
            pltpu.VMEM((1, mon_count), F32),
            pltpu.VMEM((1, mon_count), jnp.int32),
            pltpu.SMEM(outages.shape, jnp.int32),
            pltpu.VMEM(psi.shape, F32),
            pltpu.VMEM((n_out, BR_DEV, width), F32),
            pltpu.VMEM((n_mon, SEL_O, width), F32),
            pltpu.VMEM((SEL_O, width), F32),
            pltpu.VMEM((SEL_O, BR_DEV), F32),
            pltpu.VMEM((mon_count, out_count), F32),
            pltpu.VMEM((out_count, mon_count), F32),
            pltpu.VMEM((mon_count, 1), F32),
            pltpu.VMEM((mon_count, width), BF16),
            pltpu.VMEM((mon_count, width), BF16),
            pltpu.VMEM((mon_count, 1), F32),
            pltpu.VMEM((n_out, BR_DEV, width), F32),
            pltpu.VMEM((2, nz, SEL_O, width), F32),
            pltpu.VMEM((n_out, BR_DEV, width), F32),
            pltpu.VMEM((nz, SEL_O, width), F32),
            pltpu.VMEM((nz, SEL_O, width), F32),
            dma((6,)), dma((n_out - 1,)), dma((n_out,)), dma((nz,)), dma((n_mon,)),
            dma(()), dma((nz,)), dma((n_out - 1,)), dma((n_out,)),
            dma((nz,)), dma((nz,)), dma((nz,)), dma((nz,)),
        ],
        compiler_params=pltpu.CompilerParams(
            collective_id=0, has_side_effects=True, vmem_limit_bytes=40 << 20),
        name="flow_variance_grad",
    )(*[pltpu.with_memory_space_constraint(x, pltpu.HBM) for x in (psi, lodf, block_map, margin.reshape(1, -1), monitored.reshape(1, -1), outages)])


def solution(mesh):
    in_specs = (
        P(("grp", "mon", "out"), None),
        P(("grp", "mon"), "out"),
        P(("grp", "mon"), "out"),
        P(("grp", "mon")),
        P(("grp", "mon")),
        P(("grp", "out")),
    )
    out_specs = P(("grp", "mon", "out"), None)
    fn = functools.partial(body, mesh.shape["mon"], mesh.shape["out"])
    return jax.shard_map(fn, mesh=mesh, in_specs=in_specs, out_specs=out_specs, check_vma=False)
```
